256 devices in a mesh: group: 8 (over z), seq: 32 (over x, y, core).
Axes of the slice: x: 4, y: 4, z: 8, core: 2. Of those that a mesh axis runs over, the one named last changes fastest.
Arguments:
- queries: bfloat16 [8, 1024, 4096], P('group', 'seq')
- keys: bfloat16 [8, 1024, 4096], P('group', 'seq')
- values: bfloat16 [8, 1024, 4096], P('group', 'seq'), may hold values from -6 to 6
- valid: int32 [8], replicated, may hold values from 256 to 1024, as said below
- levels: int32 [8], replicated, may hold values from 0 to 63
- gate_table: float32 [64, 4096], replicated, may hold values from 0.5 to 2
Outputs:
- mixed: bfloat16 [8, 1024, 4096], P('group', 'seq')
The draws below stay inside these ranges and needn't reach their ends.
Inputs may be any that keep to these rules, and one draw needn't show every extreme that they name: Each group has at least 256 valid tokens, and at least one group has all 1024.
All inputs are finite; a program needn't handle non-finite values.
Results may differ from the reference program's by a relative error of at most 0.0075.
Values may be sent and summed in bfloat16 or wider, within the bound.
No kernel may reach another device: no remote copies, remote signals or barrier semaphores. Data moves between devices by JAX's collectives and lax.ppermute only.
A program may use at most 128 MiB of HBM per device.

```python
import math
import jax
import jax.numpy as jnp
from jax import lax

HEADS = 32
HD = 128
LEVELS = 64
S = 1024
GROUPS = 8


def draw_keys(key, part):
    local_key = jax.random.fold_in(key, 7)
    result = jnp.clip(jax.random.normal(local_key, (GROUPS, S, HEADS * HD), jnp.float32), -4.0, 4.0)
    return result.astype(jnp.bfloat16)


def draw_queries(key, part):
    local_key = jax.random.fold_in(key, 5)
    result = jnp.clip(jax.random.normal(local_key, (GROUPS, S, HEADS * HD), jnp.float32), -4.0, 4.0)
    return result.astype(jnp.bfloat16)


def draw_valid(key, part):
    key = jax.random.fold_in(key, 3)
    counts = jax.random.randint(jax.random.fold_in(key, 1), (GROUPS,), S // 4, S + 1)
    fullest = jax.random.randint(jax.random.fold_in(key, 2), (), 0, GROUPS)
    return jnp.where(jnp.arange(GROUPS) == fullest, S, counts).astype(jnp.int32)


def touch_ends(values, own_key, least, high):
    extent = values.shape
    spot = [jax.random.randint(jax.random.fold_in(own_key, axis), (), 0, extent[axis]) for axis in range(len(extent))]
    values = values.at[tuple(spot)].set(least)
    longest = extent.index(max(extent))
    spot[longest] = (spot[longest] + 1) % extent[longest]
    return values.at[tuple(spot)].set(high)


def block_scale(own_key, dims, cuts, least, high):
    level, own = 1.0, jax.random.fold_in(own_key, 6)
    for axis_at, parts in cuts:
        steps = jnp.exp(jax.random.uniform(jax.random.fold_in(own, axis_at), (parts,), jnp.float32, least / len(cuts), high / len(cuts)))
        level = level * jnp.repeat(steps, dims[axis_at] // parts).reshape([-1 if axis == axis_at else 1 for axis in range(len(dims))])
    return level


def scatter_about(stream_key, extent, scale, most, cuts=(), held_as=jnp.bfloat16):
    values = scale * jax.random.normal(stream_key, extent, jnp.float32)
    if cuts:
        values = values * block_scale(stream_key, extent, cuts, -0.22, 0.18)
    return jnp.clip(values, -most, most).astype(held_as)


def setup_inputs(seed: int = 0) -> dict:
    splits = jax.random.split(jax.random.key(seed), 7)
    return {
        "queries": draw_queries(jax.random.fold_in(splits[6], 71), 0),
        "keys": draw_keys(jax.random.fold_in(splits[6], 71), 0),
        "values": scatter_about(splits[2], (GROUPS, S, HEADS * HD), 1.0, 6.0, ((0, 8), (1, 32))),
        "valid": draw_valid(jax.random.fold_in(splits[6], 71), 0),
        "levels": touch_ends(jax.random.randint(splits[4], (GROUPS,), 0, LEVELS), jax.random.fold_in(splits[4], 1), 0, LEVELS - 1).astype(jnp.int32),
        "gate_table": jnp.clip(jax.random.uniform(splits[5], (LEVELS, HEADS * HD), jnp.float32, 0.5, 2.0), 0.5, 2.0),
    }


def one_head(operands, key_live):
    query_head, key_head, value_head = operands
    score = jnp.dot(query_head, key_head.T, preferred_element_type=jnp.float32) / math.sqrt(HD)
    score = jnp.where(key_live[None, :], score, -1e+30)
    largest = lax.optimization_barrier(jnp.max(score, axis=1, keepdims=True))
    weight = jnp.where(key_live[None, :], jnp.exp(score - largest), 0.0)
    total = lax.optimization_barrier(jnp.sum(weight, axis=1, keepdims=True))
    rounded = weight.astype(jnp.bfloat16)
    return (jnp.dot(rounded, value_head, preferred_element_type=jnp.float32) / total).astype(jnp.bfloat16)

def reference(queries, keys, values, valid, levels, gate_table):
    query_all = queries.reshape(GROUPS, S, HEADS, HD)
    key_all = keys.reshape(GROUPS, S, HEADS, HD)
    value_all = values.reshape(GROUPS, S, HEADS, HD)
    positions = jnp.arange(S, dtype=jnp.int32)
    results = []
    for group_id in range(GROUPS):
        key_part = key_all[:group_id + 1].reshape((group_id + 1) * S, HEADS, HD).transpose(1, 0, 2)
        value_part = value_all[:group_id + 1].reshape((group_id + 1) * S, HEADS, HD).transpose(1, 0, 2)
        key_live = (positions[None, :] < valid[:group_id + 1, None]).reshape(-1)
        query_part = query_all[group_id].transpose(1, 0, 2)
        attended = lax.map(lambda ops: one_head(ops, key_live), (query_part, key_part, value_part))
        attended = attended.transpose(1, 0, 2).reshape(S, HEADS * HD)
        attended = jnp.where((positions < valid[group_id])[:, None], attended, jnp.zeros_like(attended))
        gate_row = gate_table[levels[group_id]]
        results.append((attended.astype(jnp.float32) * gate_row[None, :]).astype(jnp.bfloat16))
    return jnp.stack(results)
```

```python
import functools
import math

import jax
import jax.numpy as jnp
from jax import lax
from jax.experimental import pallas as pl
from jax.experimental.pallas import tpu as pltpu
from jax.sharding import Mesh
from jax.sharding import PartitionSpec as P

HD = 128
AX = ("group", "y")
DEAD = -3.0e38
VMEM = pltpu.VMEM
MIB = 1024 * 1024


def pack_kernel(n, *refs):
    out = refs[n]
    for h in range(out.shape[0]):
        for i in range(n):
            out[h, :, i * HD : (i + 1) * HD] = refs[i][:, h * HD : (h + 1) * HD]


def pack(*arrays):
    tokens, width = arrays[0].shape
    n = len(arrays)
    return pl.pallas_call(
        functools.partial(pack_kernel, n),
        out_shape=jax.ShapeDtypeStruct((width // HD, tokens, n * HD), arrays[0].dtype),
        in_specs=[pl.BlockSpec(memory_space=VMEM)] * n,
        out_specs=pl.BlockSpec(memory_space=VMEM),
        compiler_params=pltpu.CompilerParams(vmem_limit_bytes=8 * MIB),
        name="pack",
    )(*arrays)


def attend_kernel(places, valid_ref, q_ref, *refs):
    n = len(places)
    kv_in, out_ref, kv, scores, sems = refs[:n], refs[n], refs[n + 1], refs[n + 2], refs[n + 3]
    groups, slots, rows, _ = kv.shape
    x = lax.axis_index("x")
    core = lax.axis_index("core")
    copies = []
    for i, (_, _, first, slot) in enumerate(places):
        count = kv_in[i].shape[0]
        copies.append(
            pltpu.make_async_copy(kv_in[i], kv.at[pl.ds(first, count), slot], sems.at[i])
        )
        copies[-1].start()
    lane = lax.broadcasted_iota(jnp.int32, (1, rows), 1)
    spread = (lane // 32) * 64 + lane % 32
    offset = {}
    for dist, other, _, slot in places:
        source = lax.rem(x + dist, 4)
        side = 1 - core if other else core
        offset[slot] = source * 256 + side * 32
    scale = math.log2(math.e) / math.sqrt(HD)
    for copy in copies:
        copy.wait()
    pairs = groups // 2
    for p in range(pairs):
        q = jnp.concatenate([q_ref[2 * p], q_ref[2 * p + 1]], axis=0)
        q_rows = q.shape[0]

        def score(j, most, last):
            live_count = valid_ref[j]
            for s in range(slots):
                keys = kv[j, s, :, :HD]
                part = lax.dot_general(
                    q, keys, (((1,), (1,)), ((), ())), preferred_element_type=jnp.float32
                )
                live = spread + offset[s] < live_count
                part = jnp.where(live, part, DEAD)
                if last:
                    early = lax.broadcasted_iota(jnp.int32, part.shape, 0) < q_rows // 2
                    part = jnp.where(early, DEAD, part)
                scores[j, s] = part
                most = jnp.maximum(most, part)
            return most

        most = jnp.full((q_rows, rows), DEAD, jnp.float32)
        most = lax.fori_loop(0, 2 * p + 1, lambda j, c: score(j, c, False), most)
        most = score(2 * p + 1, most, True)
        top = jnp.max(most, axis=1, keepdims=True)

        def weigh(j, state):
            acc, total = state
            for s in range(slots):
                weight = jnp.exp2((scores[j, s] - top) * scale)
                total = total + weight
                acc = acc + jnp.dot(
                    weight.astype(jnp.bfloat16),
                    kv[j, s, :, HD:],
                    preferred_element_type=jnp.float32,
                )
            return acc, total

        zero = jnp.zeros((q_rows, rows), jnp.float32)
        acc, total = lax.fori_loop(0, 2 * p + 2, weigh, (zero, zero))
        total = jnp.sum(total, axis=1, keepdims=True)
        attended = acc / total
        at = lax.broadcasted_iota(jnp.int32, (rows, 1), 0)
        at = (at // 32) * 64 + at % 32 + x * 256 + core * 32
        for half in range(2):
            c = 2 * p + half
            part = attended[half * rows : (half + 1) * rows]
            part = jnp.where(at < valid_ref[c], part, 0.0)
            out_ref[c] = part.astype(out_ref.dtype)


def attend(valid, q, arrays, places):
    groups, rows, _ = q.shape
    slots = 1 + max(place[3] for place in places)
    pairs = groups * (groups + 1) // 2 * rows * rows * slots
    return pl.pallas_call(
        functools.partial(attend_kernel, places),
        out_shape=jax.ShapeDtypeStruct(q.shape, q.dtype),
        in_specs=[pl.BlockSpec(memory_space=pltpu.SMEM), pl.BlockSpec(memory_space=VMEM)]
        + [pl.BlockSpec(memory_space=pl.ANY)] * len(arrays),
        out_specs=pl.BlockSpec(memory_space=VMEM),
        scratch_shapes=[
            pltpu.VMEM((groups, slots, rows, 2 * HD), jnp.bfloat16),
            pltpu.VMEM((groups, slots, 2 * rows, rows), jnp.float32),
            pltpu.SemaphoreType.DMA((len(arrays),)),
        ],
        compiler_params=pltpu.CompilerParams(vmem_limit_bytes=32 * MIB),
        cost_estimate=pl.CostEstimate(
            flops=4 * pairs * HD, bytes_accessed=8 * MIB, transcendentals=pairs
        ),
        name="attend",
    )(valid, q, *arrays)


def shift(value, by):
    n = lax.axis_size("x")
    return lax.ppermute(value, "x", [(i, (i + by) % n) for i in range(n)])


def swap(value):
    return lax.ppermute(value, "core", [(0, 1), (1, 0)])


def shards(queries, keys, values, valid, levels, gate_table):
    tokens, width = queries.shape[1:]
    groups = lax.axis_size("group")
    kv = lax.all_to_all(pack(keys[0], values[0]), AX, 0, 0, tiled=True)
    kv = kv.reshape(groups, -1, 2 * HD)
    q = lax.all_to_all(pack(queries[0]), AX, 0, 0, tiled=True)
    q = q.reshape(groups, -1, HD)
    half = groups // 2
    low, high = kv[:half], kv[half:]
    low_l, high_r = shift(low, 1), shift(high, -1)
    high_l, low_r = shift(high, 1), shift(low, -1)
    low_o, high_o = shift(low_l, 1), shift(high_r, -1)
    arrays, places = [], []
    for value, dist, first, chunk in (
        (kv, 0, 0, 0),
        (low_l, 3, 0, 1),
        (high_r, 1, half, 2),
        (high_l, 3, half, 1),
        (low_r, 1, 0, 2),
        (low_o, 2, 0, 3),
        (high_o, 2, half, 3),
    ):
        for other in (False, True):
            arrays.append(swap(value) if other else value)
            places.append((dist, other, first, 2 * chunk + other))
    attended = attend(valid, q, arrays, places)
    returned = lax.all_to_all(attended.reshape(-1, tokens, HD), AX, 0, 0, tiled=True)
    own = lax.axis_index("group")
    level = lax.dynamic_index_in_dim(levels, own, 0, keepdims=False)
    gate = lax.dynamic_index_in_dim(gate_table, level, 0, keepdims=True)
    mixed = returned.transpose(1, 0, 2).reshape(tokens, width).astype(jnp.float32) * gate
    return mixed.astype(jnp.bfloat16)[None]


def solution(mesh):
    fine = Mesh(mesh.devices.reshape(8, 4, 4, 2), ("group", "x", "y", "core"))
    rows = P("group", ("x", "y", "core"), None)
    return jax.shard_map(
        shards,
        mesh=fine,
        in_specs=(rows, rows, rows, P(), P(), P()),
        out_specs=rows,
        check_vma=False,
    )
```

```python
import functools
import math

import jax
import jax.numpy as jnp
from jax import lax
from jax.experimental import pallas as pl
from jax.experimental.pallas import tpu as pltpu
from jax.sharding import Mesh
from jax.sharding import PartitionSpec as P

HD = 128
AX = ("group", "y")
DEAD = -3.0e38
VMEM = pltpu.VMEM
MIB = 1024 * 1024


def pack_kernel(n, *refs):
    out, held, sems = refs[n], refs[n + 1], refs[n + 2]
    copies = [pltpu.make_async_copy(refs[i], held.at[i], sems.at[i]) for i in range(n)]
    for copy in copies:
        copy.start()
    for i in range(n):
        copies[i].wait()
        for h in range(out.shape[0]):
            out[h, :, i * HD : (i + 1) * HD] = held[i, :, h * HD : (h + 1) * HD]


def pack(*arrays):
    tokens, width = arrays[0].shape
    n = len(arrays)
    return pl.pallas_call(
        functools.partial(pack_kernel, n),
        out_shape=jax.ShapeDtypeStruct((width // HD, tokens, n * HD), arrays[0].dtype),
        in_specs=[pl.BlockSpec(memory_space=pl.ANY)] * n,
        out_specs=pl.BlockSpec(memory_space=VMEM),
        scratch_shapes=[
            pltpu.VMEM((n, tokens, width), arrays[0].dtype),
            pltpu.SemaphoreType.DMA((n,)),
        ],
        compiler_params=pltpu.CompilerParams(vmem_limit_bytes=60 * MIB),
        name="pack",
    )(*arrays)


def attend_kernel(places, first, last, valid_ref, qkv_ref, *refs):
    n = len(places)
    kv_in, refs = refs[:n], refs[n:]
    if not first:
        (acc_in, top_in, total_in), refs = refs[:3], refs[3:]
    if last:
        out_ref, refs = refs[0], refs[1:]
    else:
        (acc_out, top_out, total_out), refs = refs[:3], refs[3:]
    q_ref, kv, scores, sems = refs
    groups, chunks, _, _ = kv.shape
    rows = q_ref.shape[1]
    x = lax.axis_index("x")
    core = lax.axis_index("core")
    copies = [pltpu.make_async_copy(qkv_ref.at[:, :, pl.ds(2 * HD, HD)], q_ref, sems.at[n])]
    for i, (_, chunk, side, start) in enumerate(places):
        count = kv_in[i].shape[0]
        copies.append(
            pltpu.make_async_copy(
                kv_in[i].at[:, :, pl.ds(0, 2 * HD)],
                kv.at[pl.ds(start, count), chunk, pl.ds(side * rows, rows)],
                sems.at[i],
            )
        )
    for copy in copies:
        copy.start()
    lane = lax.broadcasted_iota(jnp.int32, (1, 2 * rows), 1)
    side = jnp.where(lane < rows, core, 1 - core)
    lane = lane % rows
    spread = (lane // 32) * 64 + lane % 32 + side * 32
    origin = {chunk: lax.rem(x + dist, 4) * 256 for dist, chunk, _, _ in places}
    live = [
        [spread + origin[c] < valid_ref[j] for c in range(chunks)] for j in range(groups)
    ]
    scale = math.log2(math.e) / math.sqrt(HD)
    early = lax.broadcasted_iota(jnp.int32, (2 * rows, 2 * rows), 0) < rows
    for copy in copies:
        copy.wait()
    for p in range(groups // 2):
        q = q_ref[2 * p : 2 * p + 2].reshape(2 * rows, HD)
        most = None
        for j in range(2 * p + 2):
            for c in range(chunks):
                part = lax.dot_general(
                    q, kv[j, c, :, :HD], (((1,), (1,)), ((), ())), preferred_element_type=jnp.float32
                )
                part = jnp.where(live[j][c], part, DEAD)
                if j == 2 * p + 1:
                    part = jnp.where(early, DEAD, part)
                scores[j, c] = part
                part = jnp.maximum(part[:, :HD], part[:, HD:])
                most = part if most is None else jnp.maximum(most, part)
        top = jnp.max(most, axis=1, keepdims=True)
        pair = slice(2 * p, 2 * p + 2)
        if not first:
            old = top_in[pair].reshape(2 * rows, HD)[:, :1]
            top = jnp.maximum(top, old)
            keep = jnp.exp2((old - top) * scale)
            acc = acc_in[pair].reshape(2 * rows, HD) * keep
            total = total_in[pair].reshape(2 * rows, HD) * keep
        else:
            acc = jnp.zeros((2 * rows, HD), jnp.float32)
            total = jnp.zeros((2 * rows, HD), jnp.float32)
        for j in range(2 * p + 2):
            for c in range(chunks):
                weight = jnp.exp2((scores[j, c] - top) * scale)
                total = total + (weight[:, :HD] + weight[:, HD:])
                acc = acc + jnp.dot(
                    weight.astype(jnp.bfloat16),
                    kv[j, c, :, HD:],
                    preferred_element_type=jnp.float32,
                )
        if last:
            attended = acc / jnp.sum(total, axis=1, keepdims=True)
            at = lax.broadcasted_iota(jnp.int32, (rows, 1), 0)
            at = (at // 32) * 64 + at % 32 + x * 256 + core * 32
            for half in range(2):
                part = attended[half * rows : (half + 1) * rows]
                part = jnp.where(at < valid_ref[2 * p + half], part, 0.0)
                out_ref[2 * p + half] = part.astype(out_ref.dtype)
        else:
            acc_out[pair] = acc.reshape(2, rows, HD)
            total_out[pair] = total.reshape(2, rows, HD)
            top_out[pair] = jnp.broadcast_to(top, acc.shape).reshape(2, rows, HD)


def attend(valid, qkv, arrays, places, state=(), last=False):
    groups, rows, _ = qkv.shape
    chunks = 1 + max(place[1] for place in places)
    pairs = groups * (groups + 1) // 2 * rows * 2 * rows * chunks
    whole = pl.BlockSpec(memory_space=VMEM)
    shape = (groups, rows, HD)
    if last:
        out_shape, out_specs = jax.ShapeDtypeStruct(shape, jnp.bfloat16), whole
    else:
        out_shape, out_specs = [jax.ShapeDtypeStruct(shape, jnp.float32)] * 3, [whole] * 3
    return pl.pallas_call(
        functools.partial(attend_kernel, places, not state, last),
        out_shape=out_shape,
        in_specs=[pl.BlockSpec(memory_space=pltpu.SMEM)]
        + [pl.BlockSpec(memory_space=pl.ANY)] * (1 + len(arrays))
        + [whole] * len(state),
        out_specs=out_specs,
        scratch_shapes=[
            pltpu.VMEM(shape, jnp.bfloat16),
            pltpu.VMEM((groups, chunks, 2 * rows, 2 * HD), jnp.bfloat16),
            pltpu.VMEM((groups, chunks, 2 * rows, 2 * rows), jnp.float32),
            pltpu.SemaphoreType.DMA((1 + len(arrays),)),
        ],
        compiler_params=pltpu.CompilerParams(vmem_limit_bytes=32 * MIB),
        cost_estimate=pl.CostEstimate(
            flops=4 * pairs * HD, bytes_accessed=4 * MIB, transcendentals=pairs
        ),
        name="attend",
    )(valid, qkv, *arrays, *state)


def shift(value, by):
    n = lax.axis_size("x")
    return lax.ppermute(value, "x", [(i, (i + by) % n) for i in range(n)])


def swap(value):
    return lax.ppermute(value, "core", [(0, 1), (1, 0)])


def shards(queries, keys, values, valid, levels, gate_table):
    tokens, width = queries.shape[1:]
    groups = lax.axis_size("group")
    qkv = lax.all_to_all(pack(keys[0], values[0], queries[0]), AX, 0, 0, tiled=True)
    qkv = qkv.reshape(groups, -1, 3 * HD)
    half = groups // 2
    low, high = qkv[:half, :, : 2 * HD], qkv[half:, :, : 2 * HD]
    low_l, high_r = shift(low, 1), shift(high, -1)
    high_l, low_r = shift(high, 1), shift(low, -1)
    state = attend(
        valid,
        qkv,
        [qkv, swap(low), swap(high)],
        [(0, 0, 0, 0), (0, 0, 1, 0), (0, 0, 1, half)],
    )
    state, low_l, high_r = lax.optimization_barrier((state, low_l, high_r))
    low_o, high_o = shift(low_l, 1), shift(high_r, -1)

    def both(*pieces):
        arrays, places = [], []
        for value, dist, chunk, first in pieces:
            arrays += [value, swap(value)]
            places += [(dist, chunk, 0, first), (dist, chunk, 1, first)]
        return arrays, places

    state = attend(
        valid,
        qkv,
        *both((low_l, 3, 0, 0), (high_l, 3, 0, half), (low_r, 1, 1, 0), (high_r, 1, 1, half)),
        state=state,
    )
    state, low_o, high_o = lax.optimization_barrier((state, low_o, high_o))
    attended = attend(
        valid, qkv, *both((low_o, 2, 0, 0), (high_o, 2, 0, half)), state=state, last=True
    )
    returned = lax.all_to_all(attended.reshape(-1, tokens, HD), AX, 0, 0, tiled=True)
    own = lax.axis_index("group")
    level = lax.dynamic_index_in_dim(levels, own, 0, keepdims=False)
    gate = lax.dynamic_index_in_dim(gate_table, level, 0, keepdims=True)
    mixed = returned.transpose(1, 0, 2).reshape(tokens, width).astype(jnp.float32) * gate
    return mixed.astype(jnp.bfloat16)[None]


def solution(mesh):
    fine = Mesh(mesh.devices.reshape(8, 4, 4, 2), ("group", "x", "y", "core"))
    rows = P("group", ("x", "y", "core"), None)
    return jax.shard_map(
        shards,
        mesh=fine,
        in_specs=(rows, rows, rows, P(), P(), P()),
        out_specs=rows,
        check_vma=False,
    )
```

```python
import functools
import math

import jax
import jax.numpy as jnp
from jax import lax
from jax.experimental import pallas as pl
from jax.experimental.pallas import tpu as pltpu
from jax.sharding import Mesh
from jax.sharding import PartitionSpec as P

HD = 128
AX = ("group", "y")
DEAD = -3.0e38
VMEM = pltpu.VMEM
MIB = 1024 * 1024


def pack_kernel(n, *refs):
    out, held, sems = refs[n], refs[n + 1], refs[n + 2]
    copies = [pltpu.make_async_copy(refs[i], held.at[i], sems.at[i]) for i in range(n)]
    for copy in copies:
        copy.start()
    for i in range(n):
        copies[i].wait()
        for h in range(out.shape[0]):
            out[h, :, i * HD : (i + 1) * HD] = held[i, :, h * HD : (h + 1) * HD]


def pack(*arrays):
    tokens, width = arrays[0].shape
    n = len(arrays)
    return pl.pallas_call(
        functools.partial(pack_kernel, n),
        out_shape=jax.ShapeDtypeStruct((width // HD, tokens, n * HD), arrays[0].dtype),
        in_specs=[pl.BlockSpec(memory_space=pl.ANY)] * n,
        out_specs=pl.BlockSpec(memory_space=VMEM),
        scratch_shapes=[
            pltpu.VMEM((n, tokens, width), arrays[0].dtype),
            pltpu.SemaphoreType.DMA((n,)),
        ],
        compiler_params=pltpu.CompilerParams(vmem_limit_bytes=60 * MIB),
        name="pack",
    )(*arrays)


def cross_kernel(dists, valid_ref, qkv_ref, far_ref, *refs):
    if dists is None:
        olds, dists = None, (0, 0)
        outs, scores = refs[:6], refs[6:]
    else:
        low_ref, high_ref = refs[:2]
        olds, outs, scores = refs[2:8], refs[8:14], refs[14:]
    own = olds is None
    groups, rows, _ = qkv_ref.shape
    half = groups // 2
    x = lax.axis_index("x")
    core = lax.axis_index("core")
    lane = lax.broadcasted_iota(jnp.int32, (1, 2 * rows), 1)
    place = lane % rows
    spread = (place // 32) * 64 + place % 32 + core * 32
    scale = math.log2(math.e) / math.sqrt(HD)
    wide = (4 * rows, 2 * rows)
    row = lax.broadcasted_iota(jnp.int32, wide, 0)
    ahead = (row % (2 * rows) < rows) & (lax.broadcasted_iota(jnp.int32, wide, 1) >= rows)

    def load(t, columns):
        if own:
            ref, at = qkv_ref, 2 * t
        elif 2 * t < half:
            ref, at = low_ref, 2 * t
        else:
            ref, at = high_ref, 2 * t - half
        return ref[at : at + 2, :, columns].reshape(2 * rows, HD)

    live = []
    for t in range(half):
        token = spread + lax.rem(x + dists[2 * t >= half], 4) * 256
        live.append(token < jnp.where(lane < rows, valid_ref[2 * t], valid_ref[2 * t + 1]))
    def queries(p):
        pair = slice(2 * p, 2 * p + 2)
        return jnp.concatenate(
            [
                qkv_ref[pair, :, 2 * HD :].reshape(2 * rows, HD),
                far_ref[pair].reshape(2 * rows, HD),
            ],
            axis=0,
        )

    def score(p, t, q, most):
        part = lax.dot_general(
            q, load(t, slice(0, HD)), (((1,), (1,)), ((), ())), preferred_element_type=jnp.float32
        )
        part = jnp.where(live[t], part, DEAD)
        if t == p:
            part = jnp.where(ahead, DEAD, part)
        scores[p % 2][t] = part
        part = jnp.maximum(part[:, :HD], part[:, HD:])
        return part if most is None else jnp.maximum(most, part)

    most = score(0, 0, queries(0), None)
    for p in range(half):
        pair = slice(2 * p, 2 * p + 2)
        top = jnp.broadcast_to(jnp.max(most, axis=1, keepdims=True), most.shape)
        if own:
            acc = jnp.zeros((4 * rows, HD), jnp.float32)
            total = jnp.zeros((4 * rows, HD), jnp.float32)
        else:
            acc, old, total = (
                jnp.concatenate(
                    [olds[i][pair].reshape(2 * rows, HD), olds[3 + i][pair].reshape(2 * rows, HD)],
                    axis=0,
                )
                for i in range(3)
            )
            top = jnp.maximum(top, old)
            keep = jnp.exp2((old - top) * scale)
            acc = acc * keep
            total = total * keep
        both = jnp.concatenate([top, top], axis=1)
        most = None
        if p + 1 < half:
            q = queries(p + 1)
            most = score(p + 1, 0, q, most)
        for t in range(p + 1):
            if p + 1 < half:
                most = score(p + 1, t + 1, q, most)
            weight = jnp.exp2((scores[p % 2][t] - both) * scale)
            total = total + (weight[:, :HD] + weight[:, HD:])
            acc = acc + jnp.dot(
                weight.astype(jnp.bfloat16),
                load(t, slice(HD, 2 * HD)),
                preferred_element_type=jnp.float32,
            )
        state = (acc, top, total)
        for i in range(2):
            mine = slice(2 * i * rows, 2 * (i + 1) * rows)
            for k, value in enumerate(state):
                outs[len(state) * i + k][pair] = value[mine].reshape(2, rows, HD)


def cross(valid, qkv, far, low=None, high=None, dists=None, state=()):
    groups, rows, _ = qkv.shape
    whole = pl.BlockSpec(memory_space=VMEM)
    arrays = [] if dists is None else [low, high]
    pairs = groups * (groups + 2) * rows * rows
    return pl.pallas_call(
        functools.partial(cross_kernel, dists),
        out_shape=[jax.ShapeDtypeStruct((groups, rows, HD), jnp.float32)] * 6,
        in_specs=[pl.BlockSpec(memory_space=pltpu.SMEM)]
        + [whole] * (2 + len(arrays) + len(state)),
        out_specs=[whole] * 6,
        scratch_shapes=[pltpu.VMEM((groups // 2, 4 * rows, 2 * rows), jnp.float32)] * 2,

        compiler_params=pltpu.CompilerParams(vmem_limit_bytes=24 * MIB),
        cost_estimate=pl.CostEstimate(
            flops=4 * pairs * HD, bytes_accessed=4 * MIB, transcendentals=pairs
        ),
        name="cross",
    )(valid, qkv, far, *arrays, *state)


def attend_kernel(sets, count_in, valid_ref, qkv_ref, *refs):
    n = sum(len(places) for places in sets)
    kv_in, refs = refs[:n], refs[n:]
    states = [refs[3 * i : 3 * i + 3] for i in range(count_in)]
    refs = refs[3 * count_in :]
    out_ref, scores, held, sems = refs[0], refs[1:3], refs[3], refs[4]
    copies = []
    groups, rows, _ = qkv_ref.shape
    x = lax.axis_index("x")
    core = lax.axis_index("core")
    lane = lax.broadcasted_iota(jnp.int32, (1, 2 * rows), 1)
    side = jnp.where(lane < rows, core, 1 - core)
    lane = lane % rows
    spread = (lane // 32) * 64 + lane % 32 + side * 32
    tiles = []
    for j in range(groups):
        at = 0
        for places in sets:
            here = {}
            for dist, side, start, count in places:
                if start <= j < start + count:
                    here[side] = (kv_in[at], j - start, dist)
                at += 1
            live = spread + lax.rem(x + here[0][2], 4) * 256 < valid_ref[j]
            tiles.append((j, here[0][:2], here[1][:2], live))

    def load(tile, columns):
        return jnp.concatenate([ref[at, :, columns] for ref, at in tile[1:3]], axis=0)

    scale = math.log2(math.e) / math.sqrt(HD)
    early = lax.broadcasted_iota(jnp.int32, (2 * rows, 2 * rows), 0) < rows
    pairs = groups // 2

    def used(p):
        return [tile for tile in tiles if tile[0] < 2 * p + 2]

    def score(p, i, most):
        if p >= pairs or i >= len(used(p)):
            return most
        tile = used(p)[i]
        part = lax.dot_general(
            qkv_ref[2 * p : 2 * p + 2, :, 2 * HD :].reshape(2 * rows, HD),
            load(tile, slice(0, HD)),
            (((1,), (1,)), ((), ())),
            preferred_element_type=jnp.float32,
        )
        part = jnp.where(tile[3], part, DEAD)
        if tile[0] == 2 * p + 1:
            part = jnp.where(early, DEAD, part)
        scores[p % 2][i] = part
        part = jnp.maximum(part[:, :HD], part[:, HD:])
        return part if most is None else jnp.maximum(most, part)

    most = None
    for i in range(len(used(0))):
        most = score(0, i, most)
    for p in range(pairs):
        pair = slice(2 * p, 2 * p + 2)
        top = jnp.broadcast_to(jnp.max(most, axis=1, keepdims=True), most.shape)
        olds = [[ref[pair].reshape(2 * rows, HD) for ref in state] for state in states]
        for _, old, _ in olds:
            top = jnp.maximum(top, old)
        acc = jnp.zeros((2 * rows, HD), jnp.float32)
        total = jnp.zeros((2 * rows, HD), jnp.float32)
        for acc_in, old, total_in in olds:
            keep = jnp.exp2((old - top) * scale)
            acc = acc + acc_in * keep
            total = total + total_in * keep
        both = jnp.concatenate([top, top], axis=1)
        most = None
        for i in range(len(tiles) // pairs):
            most = score(p + 1, i, most)
        for i, tile in enumerate(used(p)):
            most = score(p + 1, len(tiles) // pairs + i, most)
            weight = jnp.exp2((scores[p % 2][i] - both) * scale)
            total = total + (weight[:, :HD] + weight[:, HD:])
            acc = acc + jnp.dot(
                weight.astype(jnp.bfloat16),
                load(tile, slice(HD, 2 * HD)),
                preferred_element_type=jnp.float32,
            )
        attended = acc / jnp.sum(total, axis=1, keepdims=True)
        at = lax.broadcasted_iota(jnp.int32, (rows, 1), 0)
        at = (at // 32) * 64 + at % 32 + x * 256 + core * 32
        for c in (2 * p, 2 * p + 1):
            part = attended[:rows] if c == 2 * p else attended[rows:]
            part = jnp.where(at < valid_ref[c], part, 0.0)
            held[c] = part.astype(held.dtype)
        copies.append(pltpu.make_async_copy(held.at[pair], out_ref.at[pair], sems.at[p]))
        copies[-1].start()
    for copy in copies:
        copy.wait()


def attend(valid, qkv, sets, state):
    groups, rows, _ = qkv.shape
    arrays = [piece[0] for pieces in sets for piece in pieces]
    places = [[piece[1:] for piece in pieces] for pieces in sets]
    pairs = groups * (groups + 1) * rows * rows * len(sets)
    whole = pl.BlockSpec(memory_space=VMEM)
    shape = (groups, rows, HD)
    return pl.pallas_call(
        functools.partial(attend_kernel, places, len(state) // 3),
        out_shape=jax.ShapeDtypeStruct(shape, jnp.bfloat16),
        in_specs=[pl.BlockSpec(memory_space=pltpu.SMEM)]
        + [whole] * (1 + len(arrays) + len(state)),
        out_specs=pl.BlockSpec(memory_space=pltpu.HBM),
        scratch_shapes=[
            pltpu.VMEM((groups * len(sets), 2 * rows, 2 * rows), jnp.float32),
            pltpu.VMEM((groups * len(sets), 2 * rows, 2 * rows), jnp.float32),
            pltpu.VMEM(shape, jnp.bfloat16),
            pltpu.SemaphoreType.DMA((groups // 2,)),
        ],
        compiler_params=pltpu.CompilerParams(vmem_limit_bytes=24 * MIB),
        cost_estimate=pl.CostEstimate(
            flops=4 * pairs * HD, bytes_accessed=4 * MIB, transcendentals=pairs
        ),
        name="attend",
    )(valid, qkv, *arrays, *state)


def shift(value, by):
    n = lax.axis_size("x")
    return lax.ppermute(value, "x", [(i, (i + by) % n) for i in range(n)])


def swap(value):
    return lax.ppermute(value, "core", [(0, 1), (1, 0)])


def shards(queries, keys, values, valid, levels, gate_table):
    tokens, width = queries.shape[1:]
    groups = lax.axis_size("group")
    qkv = lax.all_to_all(pack(keys[0], values[0], queries[0]), AX, 0, 0, tiled=True)
    qkv = qkv.reshape(groups, -1, 3 * HD)
    half = groups // 2
    low, high = qkv[:half, :, : 2 * HD], qkv[half:, :, : 2 * HD]
    far = swap(qkv[:, :, 2 * HD :])
    low_l, high_r = shift(low, 1), shift(high, -1)
    high_l, low_r = shift(high, 1), shift(low, -1)
    state = cross(valid, qkv, far)
    state, low_l, high_r = lax.optimization_barrier((state, low_l, high_r))
    low_o, high_o = shift(low_l, 1), shift(high_r, -1)
    state = cross(valid, qkv, far, low_l, high_r, (3, 1), state)
    state, low_r, high_l = lax.optimization_barrier((state, low_r, high_l))
    state = cross(valid, qkv, far, low_r, high_l, (1, 3), state)
    rest = [
        (low_o, 2, 0, 0, half),
        (swap(low_o), 2, 1, 0, half),
        (high_o, 2, 0, half, half),
        (swap(high_o), 2, 1, half, half),
    ]
    state = [*state[:3], *(swap(part) for part in state[3:])]
    attended = attend(valid, qkv, [rest], state)
    returned = lax.all_to_all(attended.reshape(-1, tokens, HD), AX, 0, 0, tiled=True)
    own = lax.axis_index("group")
    level = lax.dynamic_index_in_dim(levels, own, 0, keepdims=False)
    gate = lax.dynamic_index_in_dim(gate_table, level, 0, keepdims=True)
    mixed = returned.transpose(1, 0, 2).reshape(tokens, width).astype(jnp.float32) * gate
    return mixed.astype(jnp.bfloat16)[None]


def solution(mesh):
    fine = Mesh(mesh.devices.reshape(8, 4, 4, 2), ("group", "x", "y", "core"))
    rows = P("group", ("x", "y", "core"), None)
    return jax.shard_map(
        shards,
        mesh=fine,
        in_specs=(rows, rows, rows, P(), P(), P()),
        out_specs=rows,
        check_vma=False,
    )
```

```python
import functools
import math

import jax
import jax.numpy as jnp
from jax import lax
from jax.experimental import pallas as pl
from jax.experimental.pallas import tpu as pltpu
from jax.sharding import Mesh
from jax.sharding import PartitionSpec as P

HD = 128
AX = ("group", "y")
DEAD = -3.0e38
VMEM = pltpu.VMEM
MIB = 1024 * 1024


def pack_kernel(n, *refs):
    out, held, packed, sems = refs[n], refs[n + 1], refs[n + 2], refs[n + 3]
    loads = [pltpu.make_async_copy(refs[i], held.at[i], sems.at[i]) for i in range(n)]
    for copy in loads:
        copy.start()
    stores = []
    for i in range(n):
        loads[i].wait()
        for h in range(out.shape[0]):
            packed[i, h] = held[i, :, h * HD : (h + 1) * HD]
        place = out.at[:, :, pl.ds(i * HD, HD)]
        stores.append(pltpu.make_async_copy(packed.at[i], place, sems.at[n + i]))
        stores[-1].start()
    for copy in stores:
        copy.wait()


def pack(*arrays):
    tokens, width = arrays[0].shape
    n = len(arrays)
    heads = width // HD
    return pl.pallas_call(
        functools.partial(pack_kernel, n),
        out_shape=jax.ShapeDtypeStruct((heads, tokens, n * HD), arrays[0].dtype),
        in_specs=[pl.BlockSpec(memory_space=pl.ANY)] * n,
        out_specs=pl.BlockSpec(memory_space=pl.ANY),
        scratch_shapes=[
            pltpu.VMEM((n, tokens, width), arrays[0].dtype),
            pltpu.VMEM((n, heads, tokens, HD), arrays[0].dtype),
            pltpu.SemaphoreType.DMA((2 * n,)),
        ],
        compiler_params=pltpu.CompilerParams(vmem_limit_bytes=60 * MIB),
        name="pack",
    )(*arrays)


def attend_kernel(dists, other, wide, count_in, last, valid_ref, qkv_ref, *refs):
    refs = list(refs)

    def take(n):
        part, refs[:] = refs[:n], refs[n:]
        return part

    sets = 2 if wide else 1
    far = take(wide)
    own = dists is None
    if own:
        dists = (0, 0)
    else:
        low_ref, high_ref = take(2)
    olds = [take(3 * sets) for _ in range(count_in)]
    if last:
        (out_ref,) = take(1)
        held, sems = refs[2:]
    else:
        outs = take(3 * sets)
    scores = refs[:2]
    groups, rows, _ = qkv_ref.shape
    half = groups // 2
    x = lax.axis_index("x")
    core = lax.axis_index("core")
    copies = []
    lane = lax.broadcasted_iota(jnp.int32, (1, 2 * rows), 1)
    place = lane % rows
    spread = (place // 32) * 64 + place % 32 + (1 - core if other else core) * 32
    scale = math.log2(math.e) / math.sqrt(HD)
    shape = (2 * sets * rows, 2 * rows)
    row = lax.broadcasted_iota(jnp.int32, shape, 0)
    ahead = (row % (2 * rows) < rows) & (lax.broadcasted_iota(jnp.int32, shape, 1) >= rows)

    def load(t, columns):
        if own:
            ref, at = qkv_ref, 2 * t
        elif 2 * t < half:
            ref, at = low_ref, 2 * t
        else:
            ref, at = high_ref, 2 * t - half
        return ref[at : at + 2, :, columns].reshape(2 * rows, HD)

    live = []
    for t in range(half):
        token = spread + lax.rem(x + dists[2 * t >= half], 4) * 256
        live.append(token < jnp.where(lane < rows, valid_ref[2 * t], valid_ref[2 * t + 1]))

    def queries(p):
        pair = slice(2 * p, 2 * p + 2)
        parts = [qkv_ref[pair, :, 2 * HD :]] + [ref[pair] for ref in far]
        return jnp.concatenate([part.reshape(2 * rows, HD) for part in parts], axis=0)

    def score(p, t, q, most):
        part = lax.dot_general(
            q, load(t, slice(0, HD)), (((1,), (1,)), ((), ())), preferred_element_type=jnp.float32
        )
        part = jnp.where(live[t], part, DEAD)
        if t == p:
            part = jnp.where(ahead, DEAD, part)
        scores[p % 2][t] = part
        part = jnp.maximum(part[:, :HD], part[:, HD:])
        return part if most is None else jnp.maximum(most, part)

    most = score(0, 0, queries(0), None)
    for p in range(half):
        pair = slice(2 * p, 2 * p + 2)
        top = jnp.broadcast_to(jnp.max(most, axis=1, keepdims=True), most.shape)
        states = [
            [
                jnp.concatenate(
                    [old[3 * i + k][pair].reshape(2 * rows, HD) for i in range(sets)], axis=0
                )
                for k in range(3)
            ]
            for old in olds
        ]
        for _, old_top, _ in states:
            top = jnp.maximum(top, old_top)
        acc = jnp.zeros((2 * sets * rows, HD), jnp.float32)
        total = jnp.zeros((2 * sets * rows, HD), jnp.float32)
        for old_acc, old_top, old_total in states:
            keep = jnp.exp2((old_top - top) * scale)
            acc = acc + old_acc * keep
            total = total + old_total * keep
        both = jnp.concatenate([top, top], axis=1)
        most = None
        if p + 1 < half:
            q = queries(p + 1)
            most = score(p + 1, 0, q, most)
        for t in range(p + 1):
            if p + 1 < half:
                most = score(p + 1, t + 1, q, most)
            weight = jnp.exp2((scores[p % 2][t] - both) * scale)
            total = total + (weight[:, :HD] + weight[:, HD:])
            acc = acc + jnp.dot(
                weight.astype(jnp.bfloat16),
                load(t, slice(HD, 2 * HD)),
                preferred_element_type=jnp.float32,
            )
        if not last:
            for i in range(sets):
                mine = slice(2 * i * rows, 2 * (i + 1) * rows)
                for k, value in enumerate((acc, top, total)):
                    outs[3 * i + k][pair] = value[mine].reshape(2, rows, HD)
            continue
        attended = acc / jnp.sum(total, axis=1, keepdims=True)
        at = lax.broadcasted_iota(jnp.int32, (rows, 1), 0)
        at = (at // 32) * 64 + at % 32 + x * 256 + core * 32
        for c in (2 * p, 2 * p + 1):
            part = attended[:rows] if c == 2 * p else attended[rows:]
            held[c] = jnp.where(at < valid_ref[c], part, 0.0).astype(held.dtype)
        copies.append(pltpu.make_async_copy(held.at[pair], out_ref.at[pair], sems.at[p]))
        copies[-1].start()
    for copy in copies:
        copy.wait()


def attend(valid, qkv, far=(), keys=(), dists=None, other=False, states=(), last=False):
    groups, rows, _ = qkv.shape
    shape = (groups, rows, HD)
    whole = pl.BlockSpec(memory_space=VMEM)
    far_off = pl.BlockSpec(memory_space=pl.ANY)
    sets = 1 + len(far)
    pairs = groups * (groups + 2) // 2 * rows * rows * sets
    score_tiles = pltpu.VMEM((groups // 2, 2 * sets * rows, 2 * rows), jnp.float32)
    scratch = [score_tiles] * 2
    arrays = [*far, *keys] + [part for state in states for part in state]
    if last:
        out_shape, out_specs = jax.ShapeDtypeStruct(shape, jnp.bfloat16), far_off
        scratch += [
            pltpu.VMEM(shape, jnp.bfloat16),
            pltpu.SemaphoreType.DMA((groups // 2,)),
        ]
    else:
        out_shape = [jax.ShapeDtypeStruct(shape, jnp.float32)] * (3 * sets)
        out_specs = [whole] * (3 * sets)
    return pl.pallas_call(
        functools.partial(attend_kernel, dists, other, len(far), len(states), last),
        out_shape=out_shape,
        in_specs=[pl.BlockSpec(memory_space=pltpu.SMEM)] + [whole] * (1 + len(arrays)),
        out_specs=out_specs,
        scratch_shapes=scratch,
        compiler_params=pltpu.CompilerParams(vmem_limit_bytes=24 * MIB),
        cost_estimate=pl.CostEstimate(
            flops=4 * pairs * HD, bytes_accessed=4 * MIB, transcendentals=pairs
        ),
        name="attend",
    )(valid, qkv, *arrays)


def shift(value, by):
    n = lax.axis_size("x")
    return lax.ppermute(value, "x", [(i, (i + by) % n) for i in range(n)])


def swap(value):
    return lax.ppermute(value, "core", [(0, 1), (1, 0)])


def shards(queries, keys, values, valid, levels, gate_table):
    tokens, width = queries.shape[1:]
    groups = lax.axis_size("group")
    qkv = lax.all_to_all(pack(keys[0], values[0], queries[0]), AX, 0, 0, tiled=True)
    qkv = qkv.reshape(groups, -1, 3 * HD)
    half = groups // 2
    low, high = qkv[:half, :, : 2 * HD], qkv[half:, :, : 2 * HD]
    far = [swap(qkv[:, :, 2 * HD :])]
    low_l, high_r = shift(low, 1), shift(high, -1)
    high_l, low_r = shift(high, 1), shift(low, -1)
    part = functools.partial(attend, valid, qkv)
    state = part(far)
    state, low_l, high_r = lax.optimization_barrier((state, low_l, high_r))
    low_o, high_o = shift(low_l, 1), shift(high_r, -1)
    state = part(far, [low_l, high_r], (3, 1), states=[state])
    state, low_r, high_l = lax.optimization_barrier((state, low_r, high_l))
    state = part(far, [low_r, high_l], (1, 3), states=[state])
    mine, sent = state[:3], [swap(value) for value in state[3:]]
    mine = part(keys=[low_o, high_o], dists=(2, 2), states=[mine])
    attended = part(
        keys=[swap(low_o), swap(high_o)],
        dists=(2, 2),
        other=True,
        states=[mine, sent],
        last=True,
    )
    returned = lax.all_to_all(attended.reshape(-1, tokens, HD), AX, 0, 0, tiled=True)
    own = lax.axis_index("group")
    level = lax.dynamic_index_in_dim(levels, own, 0, keepdims=False)
    gate = lax.dynamic_index_in_dim(gate_table, level, 0, keepdims=True)
    mixed = returned.transpose(1, 0, 2).reshape(tokens, width).astype(jnp.float32) * gate
    return mixed.astype(jnp.bfloat16)[None]


def solution(mesh):
    fine = Mesh(mesh.devices.reshape(8, 4, 4, 2), ("group", "x", "y", "core"))
    rows = P("group", ("x", "y", "core"), None)
    return jax.shard_map(
        shards,
        mesh=fine,
        in_specs=(rows, rows, rows, P(), P(), P()),
        out_specs=rows,
        check_vma=False,
    )
```

```python
import functools
import math

import jax
import jax.numpy as jnp
from jax import lax
from jax.experimental import pallas as pl
from jax.experimental.pallas import tpu as pltpu
from jax.sharding import Mesh
from jax.sharding import PartitionSpec as P

HD = 128
AX = ("group", "y")
DEAD = -3.0e38
VMEM = pltpu.VMEM
MIB = 1024 * 1024


def pack_kernel(n, *refs):
    out, held, packed, sems = refs[n], refs[n + 1], refs[n + 2], refs[n + 3]
    loads = [pltpu.make_async_copy(refs[i], held.at[i], sems.at[i]) for i in range(n)]
    for copy in loads:
        copy.start()
    stores = []
    for i in range(n):
        loads[i].wait()
        for h in range(out.shape[0]):
            packed[i, h] = held[i, :, h * HD : (h + 1) * HD]
        place = out.at[:, :, pl.ds(i * HD, HD)]
        stores.append(pltpu.make_async_copy(packed.at[i], place, sems.at[n + i]))
        stores[-1].start()
    for copy in stores:
        copy.wait()


def pack(*arrays):
    tokens, width = arrays[0].shape
    n = len(arrays)
    heads = width // HD
    return pl.pallas_call(
        functools.partial(pack_kernel, n),
        out_shape=jax.ShapeDtypeStruct((heads, tokens, n * HD), arrays[0].dtype),
        in_specs=[pl.BlockSpec(memory_space=pl.ANY)] * n,
        out_specs=pl.BlockSpec(memory_space=pl.ANY),
        scratch_shapes=[
            pltpu.VMEM((n, tokens, width), arrays[0].dtype),
            pltpu.VMEM((n, heads, tokens, HD), arrays[0].dtype),
            pltpu.SemaphoreType.DMA((2 * n,)),
        ],
        compiler_params=pltpu.CompilerParams(vmem_limit_bytes=60 * MIB),
        name="pack",
    )(*arrays)


def attend_kernel(dists, other, wide, count_in, last, valid_ref, qkv_ref, *refs):
    refs = list(refs)

    def take(n):
        part, refs[:] = refs[:n], refs[n:]
        return part

    sets = max(1, wide)
    far = take(wide > 0)
    own = dists is None
    if own:
        dists = (0, 0)
    else:
        low_ref, high_ref = take(2)
    olds = [take(3 * sets) for _ in range(count_in)]
    if last:
        (out_ref,) = take(1)
        held, sems = refs[2:]
    else:
        outs = take(3 * sets)
    scores = refs[:2]
    groups, rows, _ = qkv_ref.shape
    half = groups // 2
    x = lax.axis_index("x")
    core = lax.axis_index("core")
    copies = []
    lane = lax.broadcasted_iota(jnp.int32, (1, 2 * rows), 1)
    place = lane % rows
    spread = (place // 32) * 64 + place % 32 + (1 - core if other else core) * 32
    scale = math.log2(math.e) / math.sqrt(HD)
    shape = (2 * sets * rows, 2 * rows)
    row = lax.broadcasted_iota(jnp.int32, shape, 0)
    ahead = (row % (2 * rows) < rows) & (lax.broadcasted_iota(jnp.int32, shape, 1) >= rows)

    def load(t, columns):
        if own:
            ref, at = qkv_ref, 2 * t
        elif 2 * t < half:
            ref, at = low_ref, 2 * t
        else:
            ref, at = high_ref, 2 * t - half
        return ref[at : at + 2, :, columns].reshape(2 * rows, HD)

    live = []
    for t in range(half):
        token = spread + lax.rem(x + dists[2 * t >= half], 4) * 256
        live.append(token < jnp.where(lane < rows, valid_ref[2 * t], valid_ref[2 * t + 1]))

    def queries(p):
        pair = slice(2 * p, 2 * p + 2)
        parts = [ref[pair] for ref in far]
        if wide != 1:
            parts.insert(0, qkv_ref[pair, :, 2 * HD :])
        return jnp.concatenate([part.reshape(2 * rows, HD) for part in parts], axis=0)

    def score(p, t, q, most):
        part = lax.dot_general(
            q, load(t, slice(0, HD)), (((1,), (1,)), ((), ())), preferred_element_type=jnp.float32
        )
        part = jnp.where(live[t], part, DEAD)
        if t == p:
            part = jnp.where(ahead, DEAD, part)
        scores[p % 2][t] = part
        part = jnp.maximum(part[:, :HD], part[:, HD:])
        return part if most is None else jnp.maximum(most, part)

    most = score(0, 0, queries(0), None)
    for p in range(half):
        pair = slice(2 * p, 2 * p + 2)
        top = jnp.broadcast_to(jnp.max(most, axis=1, keepdims=True), most.shape)
        states = [
            [
                jnp.concatenate(
                    [old[3 * i + k][pair].reshape(2 * rows, HD) for i in range(sets)], axis=0
                )
                for k in range(3)
            ]
            for old in olds
        ]
        for _, old_top, _ in states:
            top = jnp.maximum(top, old_top)
        acc = jnp.zeros((2 * sets * rows, HD), jnp.float32)
        total = jnp.zeros((2 * sets * rows, HD), jnp.float32)
        for old_acc, old_top, old_total in states:
            keep = jnp.exp2((old_top - top) * scale)
            acc = acc + old_acc * keep
            total = total + old_total * keep
        both = jnp.concatenate([top, top], axis=1)
        most = None
        if p + 1 < half:
            q = queries(p + 1)
            most = score(p + 1, 0, q, most)
        for t in range(p + 1):
            if p + 1 < half:
                most = score(p + 1, t + 1, q, most)
            weight = jnp.exp2((scores[p % 2][t] - both) * scale)
            total = total + (weight[:, :HD] + weight[:, HD:])
            acc = acc + jnp.dot(
                weight.astype(jnp.bfloat16),
                load(t, slice(HD, 2 * HD)),
                preferred_element_type=jnp.float32,
            )
        if not last:
            for i in range(sets):
                mine = slice(2 * i * rows, 2 * (i + 1) * rows)
                for k, value in enumerate((acc, top, total)):
                    outs[3 * i + k][pair] = value[mine].reshape(2, rows, HD)
            continue
        attended = acc / jnp.sum(total, axis=1, keepdims=True)
        at = lax.broadcasted_iota(jnp.int32, (rows, 1), 0)
        at = (at // 32) * 64 + at % 32 + x * 256 + core * 32
        for c in (2 * p, 2 * p + 1):
            part = attended[:rows] if c == 2 * p else attended[rows:]
            held[c] = jnp.where(at < valid_ref[c], part, 0.0).astype(held.dtype)
        copies.append(pltpu.make_async_copy(held.at[pair], out_ref.at[pair], sems.at[p]))
        copies[-1].start()
    for copy in copies:
        copy.wait()


def attend(valid, qkv, far=(), wide=0, keys=(), dists=None, other=False, states=(), last=False):
    groups, rows, _ = qkv.shape
    shape = (groups, rows, HD)
    whole = pl.BlockSpec(memory_space=VMEM)
    far_off = pl.BlockSpec(memory_space=pl.ANY)
    sets = max(1, wide)
    pairs = groups * (groups + 2) // 2 * rows * rows * sets
    score_tiles = pltpu.VMEM((groups // 2, 2 * sets * rows, 2 * rows), jnp.float32)
    scratch = [score_tiles] * 2
    arrays = [*far, *keys] + [part for state in states for part in state]
    if last:
        out_shape, out_specs = jax.ShapeDtypeStruct(shape, jnp.bfloat16), far_off
        scratch += [
            pltpu.VMEM(shape, jnp.bfloat16),
            pltpu.SemaphoreType.DMA((groups // 2,)),
        ]
    else:
        out_shape = [jax.ShapeDtypeStruct(shape, jnp.float32)] * (3 * sets)
        out_specs = [whole] * (3 * sets)
    return pl.pallas_call(
        functools.partial(attend_kernel, dists, other, wide, len(states), last),
        out_shape=out_shape,
        in_specs=[pl.BlockSpec(memory_space=pltpu.SMEM)] + [whole] * (1 + len(arrays)),
        out_specs=out_specs,
        scratch_shapes=scratch,
        compiler_params=pltpu.CompilerParams(vmem_limit_bytes=24 * MIB),
        cost_estimate=pl.CostEstimate(
            flops=4 * pairs * HD, bytes_accessed=4 * MIB, transcendentals=pairs
        ),
        name="attend",
    )(valid, qkv, *arrays)


def shift(value, by):
    n = lax.axis_size("x")
    return lax.ppermute(value, "x", [(i, (i + by) % n) for i in range(n)])


def swap(value):
    return lax.ppermute(value, "core", [(0, 1), (1, 0)])


def shards(queries, keys, values, valid, levels, gate_table):
    tokens, width = queries.shape[1:]
    groups = lax.axis_size("group")
    qkv = lax.all_to_all(pack(keys[0], values[0], queries[0]), AX, 0, 0, tiled=True)
    qkv = qkv.reshape(groups, -1, 3 * HD)
    half = groups // 2
    low, high = qkv[:half, :, : 2 * HD], qkv[half:, :, : 2 * HD]
    far = [swap(qkv[:, :, 2 * HD :])]
    low_l, high_r = shift(low, 1), shift(high, -1)
    part = functools.partial(attend, valid, qkv)
    mine, low, high = lax.optimization_barrier((part(), low, high))
    high_l, low_r = shift(high, 1), shift(low, -1)
    state = [*mine, *part(far, 1)]
    state, low_l, high_r = lax.optimization_barrier((state, low_l, high_r))
    low_o, high_o = shift(low_l, 1), shift(high_r, -1)
    state = part(far, 2, [low_l, high_r], (3, 1), states=[state])
    state, low_r, high_l = lax.optimization_barrier((state, low_r, high_l))
    state = part(far, 2, [low_r, high_l], (1, 3), states=[state])
    mine, sent = state[:3], [swap(value) for value in state[3:]]
    mine = part(keys=[low_o, high_o], dists=(2, 2), states=[mine])
    attended = part(
        keys=[swap(low_o), swap(high_o)],
        dists=(2, 2),
        other=True,
        states=[mine, sent],
        last=True,
    )
    returned = lax.all_to_all(attended.reshape(-1, tokens, HD), AX, 0, 0, tiled=True)
    own = lax.axis_index("group")
    level = lax.dynamic_index_in_dim(levels, own, 0, keepdims=False)
    gate = lax.dynamic_index_in_dim(gate_table, level, 0, keepdims=True)
    mixed = returned.transpose(1, 0, 2).reshape(tokens, width).astype(jnp.float32) * gate
    return mixed.astype(jnp.bfloat16)[None]


def solution(mesh):
    fine = Mesh(mesh.devices.reshape(8, 4, 4, 2), ("group", "x", "y", "core"))
    rows = P("group", ("x", "y", "core"), None)
    return jax.shard_map(
        shards,
        mesh=fine,
        in_specs=(rows, rows, rows, P(), P(), P()),
        out_specs=rows,
        check_vma=False,
    )
```

```python
import functools
import math

import jax
import jax.numpy as jnp
from jax import lax
from jax.experimental import pallas as pl
from jax.experimental.pallas import tpu as pltpu
from jax.sharding import Mesh
from jax.sharding import PartitionSpec as P

HD = 128
AX = ("group", "y")
DEAD = -3.0e38
VMEM = pltpu.VMEM
MIB = 1024 * 1024


def pack_kernel(n, *refs):
    out, held, packed, sems = refs[n], refs[n + 1], refs[n + 2], refs[n + 3]
    loads = [pltpu.make_async_copy(refs[i], held.at[i], sems.at[i]) for i in range(n)]
    for copy in loads:
        copy.start()
    stores = []
    for i in range(n):
        loads[i].wait()
        for h in range(out.shape[0]):
            packed[i, h] = held[i, :, h * HD : (h + 1) * HD]
        place = out.at[:, :, pl.ds(i * HD, HD)]
        stores.append(pltpu.make_async_copy(packed.at[i], place, sems.at[n + i]))
        stores[-1].start()
    for copy in stores:
        copy.wait()


def pack(*arrays):
    tokens, width = arrays[0].shape
    n = len(arrays)
    heads = width // HD
    return pl.pallas_call(
        functools.partial(pack_kernel, n),
        out_shape=jax.ShapeDtypeStruct((heads, tokens, n * HD), arrays[0].dtype),
        in_specs=[pl.BlockSpec(memory_space=pl.ANY)] * n,
        out_specs=pl.BlockSpec(memory_space=pl.ANY),
        scratch_shapes=[
            pltpu.VMEM((n, tokens, width), arrays[0].dtype),
            pltpu.VMEM((n, heads, tokens, HD), arrays[0].dtype),
            pltpu.SemaphoreType.DMA((2 * n,)),
        ],
        compiler_params=pltpu.CompilerParams(vmem_limit_bytes=60 * MIB),
        name="pack",
    )(*arrays)


def attend_kernel(dists, other, wide, count_in, last, valid_ref, qkv_ref, *refs):
    refs = list(refs)

    def take(n):
        part, refs[:] = refs[:n], refs[n:]
        return part

    sets = max(1, wide)
    far = take(wide > 0)
    own = dists is None
    if own:
        dists = (0, 0)
    else:
        low_ref, high_ref = take(2)
    olds = [take(3 * sets) for _ in range(count_in)]
    if last:
        (out_ref,) = take(1)
        held, sems = refs[2:]
    else:
        outs = take(3 * sets)
    scores = refs[:2]
    groups, rows, _ = qkv_ref.shape
    half = groups // 2
    x = lax.axis_index("x")
    core = lax.axis_index("core")
    copies = []
    lane = lax.broadcasted_iota(jnp.int32, (1, 2 * rows), 1)
    place = lane % rows
    spread = (place // 32) * 64 + place % 32 + (1 - core if other else core) * 32
    scale = math.log2(math.e) / math.sqrt(HD)
    shape = (2 * sets * rows, 2 * rows)
    row = lax.broadcasted_iota(jnp.int32, shape, 0)
    ahead = (row % (2 * rows) < rows) & (lax.broadcasted_iota(jnp.int32, shape, 1) >= rows)

    def load(t, columns):
        if own:
            ref, at = qkv_ref, 2 * t
        elif 2 * t < half:
            ref, at = low_ref, 2 * t
        else:
            ref, at = high_ref, 2 * t - half
        return ref[at : at + 2, :, columns].reshape(2 * rows, HD)

    live = []
    for t in range(half):
        token = spread + lax.rem(x + dists[2 * t >= half], 4) * 256
        live.append(token < jnp.where(lane < rows, valid_ref[2 * t], valid_ref[2 * t + 1]))

    def queries(p):
        pair = slice(2 * p, 2 * p + 2)
        parts = [ref[pair] for ref in far]
        if wide != 1:
            parts.insert(0, qkv_ref[pair, :, 2 * HD :])
        return jnp.concatenate([part.reshape(2 * rows, HD) for part in parts], axis=0)

    def score(p, t, q, most):
        part = lax.dot_general(
            q, load(t, slice(0, HD)), (((1,), (1,)), ((), ())), preferred_element_type=jnp.float32
        )
        part = jnp.where(live[t], part, DEAD)
        if t == p:
            part = jnp.where(ahead, DEAD, part)
        scores[p % 2][t] = part
        part = jnp.maximum(part[:, :HD], part[:, HD:])
        return part if most is None else jnp.maximum(most, part)

    most = score(0, 0, queries(0), None)
    for p in range(half):
        pair = slice(2 * p, 2 * p + 2)
        top = jnp.broadcast_to(jnp.max(most, axis=1, keepdims=True), most.shape)
        states = [
            [
                jnp.concatenate(
                    [old[3 * i + k][pair].reshape(2 * rows, HD) for i in range(sets)], axis=0
                )
                for k in range(3)
            ]
            for old in olds
        ]
        for _, old_top, _ in states:
            top = jnp.maximum(top, old_top)
        acc = jnp.zeros((2 * sets * rows, HD), jnp.float32)
        total = jnp.zeros((2 * sets * rows, HD), jnp.float32)
        for old_acc, old_top, old_total in states:
            keep = jnp.exp2((old_top - top) * scale)
            acc = acc + old_acc * keep
            total = total + old_total * keep
        both = jnp.concatenate([top, top], axis=1)
        most = None
        if p + 1 < half:
            q = queries(p + 1)
            most = score(p + 1, 0, q, most)
        for t in range(p + 1):
            if p + 1 < half:
                most = score(p + 1, t + 1, q, most)
            weight = jnp.exp2((scores[p % 2][t] - both) * scale)
            total = total + (weight[:, :HD] + weight[:, HD:])
            acc = acc + jnp.dot(
                weight.astype(jnp.bfloat16),
                load(t, slice(HD, 2 * HD)),
                preferred_element_type=jnp.float32,
            )
        if not last:
            for i in range(sets):
                mine = slice(2 * i * rows, 2 * (i + 1) * rows)
                for k, value in enumerate((acc, top, total)):
                    outs[3 * i + k][pair] = value[mine].reshape(2, rows, HD)
            continue
        attended = acc / jnp.sum(total, axis=1, keepdims=True)
        at = lax.broadcasted_iota(jnp.int32, (rows, 1), 0)
        at = (at // 32) * 64 + at % 32 + x * 256 + core * 32
        for c in (2 * p, 2 * p + 1):
            part = attended[:rows] if c == 2 * p else attended[rows:]
            held[c] = jnp.where(at < valid_ref[c], part, 0.0).astype(held.dtype)
        copies.append(pltpu.make_async_copy(held.at[pair], out_ref.at[pair], sems.at[p]))
        copies[-1].start()
    for copy in copies:
        copy.wait()


def attend(valid, qkv, far=(), wide=0, keys=(), dists=None, other=False, states=(), last=False):
    groups, rows, _ = qkv.shape
    shape = (groups, rows, HD)
    whole = pl.BlockSpec(memory_space=VMEM)
    far_off = pl.BlockSpec(memory_space=pl.ANY)
    sets = max(1, wide)
    pairs = groups * (groups + 2) // 2 * rows * rows * sets
    score_tiles = pltpu.VMEM((groups // 2, 2 * sets * rows, 2 * rows), jnp.float32)
    scratch = [score_tiles] * 2
    arrays = [*far, *keys] + [part for state in states for part in state]
    if last:
        out_shape, out_specs = jax.ShapeDtypeStruct(shape, jnp.bfloat16), far_off
        scratch += [
            pltpu.VMEM(shape, jnp.bfloat16),
            pltpu.SemaphoreType.DMA((groups // 2,)),
        ]
    else:
        out_shape = [jax.ShapeDtypeStruct(shape, jnp.float32)] * (3 * sets)
        out_specs = [whole] * (3 * sets)
    return pl.pallas_call(
        functools.partial(attend_kernel, dists, other, wide, len(states), last),
        out_shape=out_shape,
        in_specs=[pl.BlockSpec(memory_space=pltpu.SMEM)] + [whole] * (1 + len(arrays)),
        out_specs=out_specs,
        scratch_shapes=scratch,
        compiler_params=pltpu.CompilerParams(vmem_limit_bytes=24 * MIB),
        cost_estimate=pl.CostEstimate(
            flops=4 * pairs * HD, bytes_accessed=4 * MIB, transcendentals=pairs
        ),
        name="attend",
    )(valid, qkv, *arrays)


def shift(value, by):
    n = lax.axis_size("x")
    return lax.ppermute(value, "x", [(i, (i + by) % n) for i in range(n)])


def swap(value):
    return lax.ppermute(value, "core", [(0, 1), (1, 0)])


def finish_kernel(heads_ref, gate_ref, out_ref):
    for h in range(heads_ref.shape[0]):
        columns = slice(h * HD, (h + 1) * HD)
        mixed = heads_ref[h].astype(jnp.float32) * gate_ref[:, columns]
        out_ref[:, columns] = mixed.astype(out_ref.dtype)


def finish(heads, gate):
    count, tokens, _ = heads.shape
    return pl.pallas_call(
        finish_kernel,
        out_shape=jax.ShapeDtypeStruct((tokens, count * HD), heads.dtype),
        in_specs=[pl.BlockSpec(memory_space=VMEM)] * 2,
        out_specs=pl.BlockSpec(memory_space=VMEM),
        compiler_params=pltpu.CompilerParams(vmem_limit_bytes=8 * MIB),
        name="finish",
    )(heads, gate)


def shards(queries, keys, values, valid, levels, gate_table):
    tokens, width = queries.shape[1:]
    groups = lax.axis_size("group")
    qkv = lax.all_to_all(pack(keys[0], values[0], queries[0]), AX, 0, 0, tiled=True)
    qkv = qkv.reshape(groups, -1, 3 * HD)
    half = groups // 2
    low, high = qkv[:half, :, : 2 * HD], qkv[half:, :, : 2 * HD]
    far = [swap(qkv[:, :, 2 * HD :])]
    low_l, high_r = shift(low, 1), shift(high, -1)
    part = functools.partial(attend, valid, qkv)
    mine, low, high = lax.optimization_barrier((part(), low, high))
    high_l, low_r = shift(high, 1), shift(low, -1)
    state = [*mine, *part(far, 1)]
    state, low_l, high_r = lax.optimization_barrier((state, low_l, high_r))
    low_o, high_o = shift(low_l, 1), shift(high_r, -1)
    state = part(far, 2, [low_l, high_r], (3, 1), states=[state])
    state, low_r, high_l = lax.optimization_barrier((state, low_r, high_l))
    state = part(far, 2, [low_r, high_l], (1, 3), states=[state])
    mine, sent = state[:3], [swap(value) for value in state[3:]]
    mine = part(keys=[low_o, high_o], dists=(2, 2), states=[mine])
    attended = part(
        keys=[swap(low_o), swap(high_o)],
        dists=(2, 2),
        other=True,
        states=[mine, sent],
        last=True,
    )
    returned = lax.all_to_all(attended.reshape(-1, tokens, HD), AX, 0, 0, tiled=True)
    own = lax.axis_index("group")
    level = lax.dynamic_index_in_dim(levels, own, 0, keepdims=False)
    gate = lax.dynamic_index_in_dim(gate_table, level, 0, keepdims=True)
    return finish(returned, gate)[None]


def solution(mesh):
    fine = Mesh(mesh.devices.reshape(8, 4, 4, 2), ("group", "x", "y", "core"))
    rows = P("group", ("x", "y", "core"), None)
    return jax.shard_map(
        shards,
        mesh=fine,
        in_specs=(rows, rows, rows, P(), P(), P()),
        out_specs=rows,
        check_vma=False,
    )
```
